32 devices in a mesh: groups: 2 (over y), node: 4 (over z), tensor: 2 (over x), pair: 2 (over core).
Axes of the slice: x: 2, y: 2, z: 4, core: 2. Of those that a mesh axis runs over, the one named last changes fastest.
Arguments:
- attention_partial: bfloat16 [4, 128, 6144], P(('tensor', 'pair'), ('groups', 'node')), parts along dimension 1, may hold values from -4 to 4
- residual: bfloat16 [8, 4, 4, 6144], P(('groups', 'node'), ('tensor', 'pair')), parts along dimension 0, may hold values from -6 to 6
- norm_scale: bfloat16 [6144], replicated, may hold values from 0.099609375 to 1.8984375
- router_matrix: bfloat16 [6144, 4], replicated, may hold values from -0.078125 to 0.078125
- up_matrix: bfloat16 [4, 6144, 8192], P('node', None, ('tensor', 'pair')), may hold values from -0.078125 to 0.078125
- down_matrix: bfloat16 [4, 8192, 6144], P('node', None, ('tensor', 'pair')), may hold values from -0.0625 to 0.0625
- adapter_in_maps: bfloat16 [4, 4, 6144, 16], P(None, None, ('tensor', 'pair')), may hold values from -0.078125 to 0.078125
- adapter_out_maps: bfloat16 [4, 4, 16, 8192], P(None, 'node', None, ('tensor', 'pair')), may hold values from -1.5 to 1.5
- token_experts: int32 [8, 4, 4, 2], P(('groups', 'node'), ('tensor', 'pair')), parts along dimension 0, may hold values from 0 to 3, as said below
- token_requests: int32 [8, 4, 4], P(('groups', 'node'), ('tensor', 'pair')), parts along dimension 0, may hold values from 0 to 7, as said below
- request_adapters: int32 [16], P('groups'), parts along dimension 0, may hold values from 0 to 3
Outputs:
- mixed: bfloat16 [8, 4, 4, 6144], P(('groups', 'node'), ('tensor', 'pair')), parts along dimension 0
The draws below stay inside these ranges and needn't reach their ends.
There are 2 independent parts, one for each index of `groups`. The reference program is written for one: setup_inputs(seed, part) draws one part's arguments, and reference() takes and returns one part's arrays. A program takes and returns all parts, laid end to end along the dimension named above; an argument that names none is the same for every part. Nothing has to cross between parts.
Inputs may be any that keep to these rules, and one draw needn't show every extreme that they name: `token_experts`: each token names two different experts. In every aligned block of 4 tokens (the tokens of one device), the experts are named by 3, 2, 2 and 1 tokens in some order. `token_requests`: never falling along the tokens; every request has one or more tokens.
All inputs are finite; a program needn't handle non-finite values.
Results may differ from the reference program's by a relative error of at most 0.013.
Values may be sent and summed in bfloat16 or wider, within the bound.
A program may use at most 128 MiB of HBM per device.

```python
import jax
import jax.numpy as jnp
from jax import lax

MODEL_DIM = 6144
FF = 8192
EXPERT_COUNT = 4
ADAPTER_RANK = 16
ADAPTER_COUNT = 4
REQUESTS = 8
TOK_DEV = 4
HEAD_GROUPS = 4
BLOCKS = 4
TOKENS = 64
NODE_SHARE = 1
HIDDEN_PER_NODE = 8192
N_NODE = 4


def draw_token_experts(key, part):
    key = jax.random.fold_in(key, 11)
    count = BLOCKS * HEAD_GROUPS
    keys = jax.random.split(key, 6)
    ranking = jax.random.permutation(keys[0], EXPERT_COUNT)
    table = jnp.array([0, 0, 0, 0, 1, 1, 2, 3], jnp.int32)
    heavy = ranking[table[jax.random.randint(keys[1], (count,), 0, 8)]]
    free_row = jax.random.randint(keys[2], (count,), 0, TOK_DEV)
    shifts = jax.vmap(lambda single: jax.random.permutation(single, 3))(jax.random.split(keys[3], count)) + 1
    skipped = jax.random.randint(keys[4], (count,), 1, 4)
    flips = jax.random.randint(keys[5], (count, TOK_DEV), 0, 2)
    row_index = jnp.arange(TOK_DEV)[None, :]
    is_free = row_index == free_row[:, None]
    ranked = row_index - (row_index > free_row[:, None]).astype(jnp.int32)
    ranked = jnp.minimum(ranked, 2)
    other = jnp.take_along_axis(shifts, ranked, axis=1)
    first = jnp.where(is_free, heavy[:, None] + (skipped % 3 + 1)[:, None], heavy[:, None] + 0 * row_index)
    second = jnp.where(is_free, heavy[:, None] + ((skipped + 1) % 3 + 1)[:, None], heavy[:, None] + other)
    first = first % EXPERT_COUNT
    second = second % EXPERT_COUNT
    lead = jnp.where(flips == 1, second, first)
    trail = jnp.where(flips == 1, first, second)
    result = jnp.stack([lead, trail], axis=2).astype(jnp.int32)
    return result.reshape(BLOCKS, HEAD_GROUPS, TOK_DEV, 2)


def draw_token_requests(key, part):
    key = jax.random.fold_in(key, 23)
    cuts = jax.random.permutation(key, TOKENS - 1)[:REQUESTS - 1] + 1
    position = jnp.arange(TOKENS)
    segment = jnp.sum((position[:, None] >= cuts[None, :]).astype(jnp.int32), axis=1).astype(jnp.int32)
    return segment.reshape(BLOCKS, HEAD_GROUPS, TOK_DEV)


def with_ends(values, stream_key, low, largest):
    longest = values.shape.index(max(values.shape))
    spots = []
    for shift in (0, 1):
        where = [jax.random.randint(jax.random.fold_in(stream_key, axis), (), 0, length) for axis, length in enumerate(values.shape)]
        where[longest] = (where[longest] + shift) % values.shape[longest]
        spots.append(tuple(where))
    return values.at[spots[0]].set(low).at[spots[1]].set(largest)


def level_of(stream_key, extent, pieces, least, top_value):
    factor_of, own = 1.0, jax.random.fold_in(stream_key, 6)
    for axis_at, parts in pieces:
        heights = jnp.exp(jax.random.uniform(jax.random.fold_in(own, axis_at), (parts,), jnp.float32, least / len(pieces), top_value / len(pieces)))
        factor_of = factor_of * jnp.repeat(heights, extent[axis_at] // parts).reshape([-1 if axis == axis_at else 1 for axis in range(len(extent))])
    return factor_of


def noise(own_key, dims, scale, most, shards=(), dtype=jnp.bfloat16):
    values = jax.random.normal(own_key, dims, jnp.float32) * scale
    if len(shards) > 0:
        values = level_of(own_key, dims, shards, -0.22, 0.18) * values
    return jnp.clip(values, min=-most, max=most).astype(dtype)


def setup_inputs(seed: int = 0, part: int = 0) -> dict:
    splits = jax.random.split(jax.random.key(seed), 12)
    own_keys = jax.random.split(jax.random.fold_in(splits[11], part), 12)
    return {
        "attention_partial": noise(own_keys[0], (HEAD_GROUPS, TOKENS, MODEL_DIM), 0.5, 4.0, ((0, 4), (1, 4))),
        "residual": noise(own_keys[1], (BLOCKS, HEAD_GROUPS, TOK_DEV, MODEL_DIM), 1.0, 6.0, ((0, 4), (1, 4))),
        "norm_scale": jnp.clip(1.0 + 0.18 * jax.random.normal(splits[2], (MODEL_DIM,), jnp.float32), 0.099609375, 1.8984375).astype(jnp.bfloat16),
        "router_matrix": noise(splits[3], (MODEL_DIM, EXPERT_COUNT), MODEL_DIM ** -0.5, 0.078125),
        "up_matrix": noise(splits[4], (N_NODE, MODEL_DIM, HIDDEN_PER_NODE), MODEL_DIM ** -0.5, 0.078125, ((0, 4), (2, 4))),
        "down_matrix": noise(splits[5], (N_NODE, HIDDEN_PER_NODE, MODEL_DIM), FF ** -0.5, 0.0625, ((0, 4), (2, 4))),
        "adapter_in_maps": noise(splits[6], (ADAPTER_COUNT, EXPERT_COUNT, MODEL_DIM, ADAPTER_RANK), MODEL_DIM ** -0.5, 0.078125, ((2, 4),)),
        "adapter_out_maps": noise(splits[7], (ADAPTER_COUNT, N_NODE, ADAPTER_RANK, HIDDEN_PER_NODE), ADAPTER_RANK ** -0.5, 1.5, ((1, 4), (3, 4))),
        "token_experts": draw_token_experts(jax.random.fold_in(jax.random.fold_in(splits[11], part), 71), part),
        "token_requests": draw_token_requests(jax.random.fold_in(jax.random.fold_in(splits[11], part), 71), part),
        "request_adapters": with_ends(jax.random.randint(own_keys[10], (REQUESTS,), 0, ADAPTER_COUNT), jax.random.fold_in(own_keys[10], 1), 0, ADAPTER_COUNT - 1).astype(jnp.int32),
    }


def silu_value(value):
    return value / (1.0 + jnp.exp(-value))

def reference(attention_partial, residual, norm_scale, router_matrix, up_matrix, down_matrix, adapter_in_maps, adapter_out_maps, token_experts, token_requests, request_adapters):
    head_total = residual.reshape(TOKENS, MODEL_DIM).astype(jnp.float32) + lax.optimization_barrier(jnp.sum(attention_partial.astype(jnp.float32), axis=0))
    mean_square = lax.optimization_barrier(jnp.mean(head_total * head_total, axis=1, keepdims=True))
    normalized_input = (head_total * lax.rsqrt(mean_square + 1e-05) * norm_scale.astype(jnp.float32)).astype(jnp.bfloat16)
    logits = jnp.dot(normalized_input, router_matrix, preferred_element_type=jnp.float32)
    routes = token_experts.reshape(TOKENS, 2)
    chosen = jnp.take_along_axis(logits, routes, axis=1)
    first_gate = 1.0 / (1.0 + jnp.exp(chosen[:, 1] - chosen[:, 0]))
    gates = jnp.stack([first_gate, 1.0 - first_gate], axis=1)
    adapter = request_adapters[token_requests.reshape(TOKENS)]
    adapter_choice = (adapter[:, None] == jnp.arange(ADAPTER_COUNT)[None, :]).astype(jnp.float32)
    moe_total = jnp.zeros((TOKENS, MODEL_DIM), jnp.float32)
    for expert_index in range(EXPERT_COUNT):
        weight_e = lax.optimization_barrier(jnp.sum(gates * (routes == expert_index).astype(jnp.float32), axis=1))
        middle_sum = jnp.zeros((TOKENS, ADAPTER_RANK), jnp.float32)
        for which_slot in range(ADAPTER_COUNT):
            middle_sum = middle_sum + adapter_choice[:, which_slot:which_slot + 1] * jnp.dot(normalized_input, adapter_in_maps[which_slot, expert_index], preferred_element_type=jnp.float32)
        adapter_middle = middle_sum.astype(jnp.bfloat16)
        expert_sum = jnp.zeros((TOKENS, MODEL_DIM), jnp.float32)
        for block in range(NODE_SHARE):
            node_row_index = expert_index * NODE_SHARE + block
            up_projection = jnp.dot(normalized_input, up_matrix[node_row_index], preferred_element_type=jnp.float32)
            for which_slot in range(ADAPTER_COUNT):
                up_projection = up_projection + adapter_choice[:, which_slot:which_slot + 1] * jnp.dot(adapter_middle, adapter_out_maps[which_slot, node_row_index], preferred_element_type=jnp.float32)
            hidden = silu_value(up_projection).astype(jnp.bfloat16)
            piece = jnp.dot(hidden, down_matrix[node_row_index], preferred_element_type=jnp.float32).astype(jnp.bfloat16)
            expert_sum = expert_sum + piece.astype(jnp.float32)
        moe_total = moe_total + weight_e[:, None] * expert_sum
    mixed = (head_total + moe_total).astype(jnp.bfloat16)
    return mixed.reshape(BLOCKS, HEAD_GROUPS, TOK_DEV, MODEL_DIM)
```

```python
import functools

import jax
import jax.numpy as jnp
from jax import lax
from jax.experimental import pallas as pl
from jax.experimental.pallas import tpu as pltpu
from jax.sharding import PartitionSpec as P

EXPERT_COUNT = 4
MESH = pl.DeviceIdType.MESH
F32 = jnp.float32
BF16 = jnp.bfloat16


def kernel(
    dims,
    ap_ref,
    res_ref,
    scale_ref,
    router_ref,
    up_ref,
    down_ref,
    in_ref,
    outmap_ref,
    te_ref,
    tr_ref,
    ra_ref,
    out_ref,
    w_up,
    w_down,
    a_in,
    ap_buf,
    res_buf,
    head,
    y_buf,
    inf_buf,
    inf_all,
    part_buf,
    meta,
    lora_buf,
    acc,
    hid,
    acc_down,
    piece,
    ret,
    outb,
    up_sem,
    down_sem,
    loc_sem,
    ap_s,
    ap_r,
    res_s,
    res_r,
    inf_s,
    inf_r,
    part_s,
    part_r,
    meta_s,
    meta_r,
    z_s,
    z_r,
    x_s,
    x_r,
    p_s,
    p_r,
    lora_s,
    lora_r,
    hx_s,
    hx_r,
    hp_s,
    hp_r,
    ret_s,
    ret_r,
    out_s,
    out_r,
):
    nodes, tensors, groups, own, block, cols, width, chunks, chunk, rank, adapters, share = dims
    z = lax.axis_index("node")
    t = lax.axis_index("tensor")
    p = lax.axis_index("pair")
    c = t * 2 + p
    q = 1 - p
    tokens = nodes * block

    def at_cols(index):
        return pl.ds(pl.multiple_of(index * cols, cols), cols)

    def at_block(index):
        return pl.ds(pl.multiple_of(index * block, block), block)

    def to_chip(index):
        return {"tensor": index // 2, "pair": lax.rem(index, 2)}

    def remote(src, dst, send, recv, device):
        return pltpu.make_async_remote_copy(
            src_ref=src, dst_ref=dst, send_sem=send, recv_sem=recv,
            device_id=device, device_id_type=MESH,
        )

    chip_to = [lax.rem(c + d, groups) for d in range(1, groups)]
    chip_from = [lax.rem(c - d + groups, groups) for d in range(1, groups)]
    node_to = [lax.rem(z + d, nodes) for d in range(1, nodes)]
    node_from = [lax.rem(z - d + nodes, nodes) for d in range(1, nodes)]
    tens_to = [lax.rem(t + d, tensors) for d in range(1, tensors)]
    tens_from = [lax.rem(t - d + tensors, tensors) for d in range(1, tensors)]
    sends = []

    def go(copy):
        copy.start()
        sends.append(copy)

    def up_copy(index):
        rows = at_cols(index)
        return pltpu.make_async_copy(up_ref.at[rows], w_up.at[rows], up_sem.at[index])

    def down_copy(index):
        rows = pl.ds(pl.multiple_of(index * width, width), width)
        return pltpu.make_async_copy(down_ref.at[rows], w_down.at[rows], down_sem.at[index])

    order = [c, t * 2 + q]
    for t2 in tens_from:
        order.append(t2 * 2 + p)
    for t2 in tens_from:
        order.append(t2 * 2 + q)

    own_ap = pltpu.make_async_copy(ap_ref.at[:, at_cols(c)], ap_buf.at[c], loc_sem.at[0])
    own_ap.start()
    in_copy = pltpu.make_async_copy(in_ref.at[:, z // share], a_in, loc_sem.at[1])
    in_copy.start()
    for index in order:
        up_copy(index).start()

    barrier = pltpu.get_barrier_semaphore()
    for c2 in chip_to:
        pl.semaphore_signal(barrier, inc=1, device_id=to_chip(c2), device_id_type=MESH)
    for z2 in node_to:
        pl.semaphore_signal(barrier, inc=1, device_id={"node": z2}, device_id_type=MESH)

    row8 = lax.broadcasted_iota(jnp.int32, (8, 128), 0)
    lane8 = lax.broadcasted_iota(jnp.int32, (8, 128), 1)
    info = jnp.zeros((8, 128), jnp.int32)
    for k in range(own):
        here = row8 == k
        info = jnp.where(here & (lane8 == 0), ra_ref[tr_ref[k]], info)
        info = jnp.where(here & (lane8 == 1), te_ref[k, 0], info)
        info = jnp.where(here & (lane8 == 2), te_ref[k, 1], info)
    inf_buf[c] = info

    pl.semaphore_wait(barrier, groups - 1 + nodes - 1)

    for c2 in chip_to:
        go(remote(ap_ref.at[:, at_cols(c2)], ap_buf.at[c], ap_s.at[c2], ap_r.at[c], to_chip(c2)))
    for c2 in chip_to:
        go(remote(res_ref.at[:, at_cols(c2)], res_buf.at[c], res_s.at[c2], res_r.at[c], to_chip(c2)))
    for c2 in chip_to:
        go(remote(inf_buf.at[c], inf_buf.at[c], inf_s.at[c2], inf_r.at[c], to_chip(c2)))

    res_buf[c] = res_ref[:, at_cols(c)]
    for c2 in chip_from:
        remote(res_buf.at[c2], res_buf.at[c2], res_s.at[c2], res_r.at[c2], to_chip(c2)).wait_recv()
    for index in range(groups):
        head[index * own : (index + 1) * own, :] = res_buf[index].astype(F32)
    own_ap.wait()
    for c2 in chip_from:
        remote(ap_buf.at[c2], ap_buf.at[c2], ap_s.at[c2], ap_r.at[c2], to_chip(c2)).wait_recv()
    total = ap_buf[0].astype(F32)
    for index in range(1, groups):
        total = total + ap_buf[index].astype(F32)
    total = total + head[...]
    head[...] = total
    scale = scale_ref[:, at_cols(c)].astype(F32)
    y = (total * scale).astype(BF16)
    y_buf[c, at_block(z), :] = y

    def z_copy(z2, who):
        piece_ref = y_buf.at[c, at_block(who)]
        return remote(piece_ref, piece_ref, z_s.at[z2], z_r.at[who], {"node": z2})

    def x_copy(t2, who_t, zb):
        piece_ref = y_buf.at[who_t * 2 + p, at_block(zb)]
        return remote(piece_ref, piece_ref, x_s.at[t2, zb], x_r.at[who_t, zb], {"tensor": t2})

    def p_copy(t2, core, zb):
        piece_ref = y_buf.at[t2 * 2 + core, at_block(zb)]
        return remote(piece_ref, piece_ref, p_s.at[t2, zb], p_r.at[t2, zb], {"pair": q})

    def spread(zb):
        for t2 in tens_to:
            go(x_copy(t2, t, zb))
        go(p_copy(t, p, zb))

    for z2 in node_to:
        go(z_copy(z2, z))
    spread(z)

    lane = lax.broadcasted_iota(jnp.int32, (block, 128), 1)
    y32 = y.astype(F32)
    router = router_ref[:, at_cols(c)].astype(F32)
    partial = jnp.where(lane == 0, jnp.sum(total * total, axis=1, keepdims=True), 0.0)
    for e in range(EXPERT_COUNT):
        value = jnp.sum(y32 * router[e : e + 1, :], axis=1, keepdims=True)
        partial = jnp.where(lane == 1 + e, value, partial)
    part_buf[c] = partial
    for c2 in chip_to:
        go(remote(part_buf.at[c], part_buf.at[c], part_s.at[c2], part_r.at[c], to_chip(c2)))
    for index in order:
        down_copy(index).start()
    for c2 in chip_from:
        remote(inf_buf.at[c2], inf_buf.at[c2], inf_s.at[c2], inf_r.at[c2], to_chip(c2)).wait_recv()
    for index in range(groups):
        inf_all[index * own : (index + 1) * own, :] = inf_buf[index, 0:own, :]
    for c2 in chip_from:
        remote(part_buf.at[c2], part_buf.at[c2], part_s.at[c2], part_r.at[c2], to_chip(c2)).wait_recv()
    sums = part_buf[0]
    for index in range(1, groups):
        sums = sums + part_buf[index]
    root = lax.rsqrt(sums[:, 0:1] / (groups * cols) + 1e-05)
    routes = inf_all[...]
    meta[z] = jnp.where(
        lane == 0, root, jnp.where(lane == 1, routes[:, 0:1].astype(F32), 0.0)
    )
    for z2 in node_to:
        go(remote(meta.at[z], meta.at[z], meta_s.at[z2], meta_r.at[z], {"node": z2}))
    first_expert = routes[:, 1:2]
    second_expert = routes[:, 2:3]
    chosen0 = jnp.zeros((block, 1), F32)
    chosen1 = jnp.zeros((block, 1), F32)
    for e in range(EXPERT_COUNT):
        logit = sums[:, 1 + e : 2 + e] * root
        chosen0 = jnp.where(first_expert == e, logit, chosen0)
        chosen1 = jnp.where(second_expert == e, logit, chosen1)
    gate0 = 1.0 / (1.0 + jnp.exp(chosen1 - chosen0))
    gate1 = 1.0 - gate0

    for z2 in node_from:
        z_copy(z2, z2).wait_recv()
        spread(z2)

    in_copy.wait()
    wide = adapters * rank
    mid = lax.dot_general(
        y_buf[c], a_in[...].reshape(wide, cols), (((1,), (1,)), ((), ())),
        preferred_element_type=F32,
    )
    lora_buf[c] = mid.astype(BF16)
    for c2 in chip_to:
        go(remote(lora_buf.at[c], lora_buf.at[c], lora_s.at[c2], lora_r.at[c], to_chip(c2)))

    def up_part(index, j):
        lanes = pl.ds(pl.multiple_of(j * chunk, chunk), chunk)
        rows = at_cols(index)
        return jnp.dot(y_buf[index], w_up[rows, lanes], preferred_element_type=F32)

    def up_step(index, first):
        up_copy(index).wait()

        def body(j, carry):
            value = up_part(index, j)
            acc[j] = value if first else acc[j] + value
            return carry

        lax.fori_loop(0, chunks, body, 0)

    up_step(order[0], True)
    for zb in range(nodes):
        p_copy(t, q, zb).wait_recv()
    up_step(order[1], False)
    for t2 in tens_from:
        for zb in [z] + node_from:
            x_copy(t2, t2, zb).wait_recv()
            go(p_copy(t2, p, zb))
        up_step(t2 * 2 + p, False)

    for c2 in chip_from:
        remote(lora_buf.at[c2], lora_buf.at[c2], lora_s.at[c2], lora_r.at[c2], to_chip(c2)).wait_recv()
    for z2 in node_from:
        remote(meta.at[z2], meta.at[z2], meta_s.at[z2], meta_r.at[z2], {"node": z2}).wait_recv()
    facts = meta[...].reshape(tokens, 128)
    root_all = facts[:, 0:1]
    low = facts[:, 1:2] * float(rank)
    mid = lora_buf[0].astype(F32)
    for index in range(1, groups):
        mid = mid + lora_buf[index].astype(F32)
    slot = lax.broadcasted_iota(jnp.int32, (tokens, wide), 1).astype(F32)
    mid = jnp.where((slot >= low) & (slot < low + rank), mid * root_all, 0.0).astype(BF16)

    last = [t2 * 2 + q for t2 in tens_from]
    for i, t2 in enumerate(tens_from):
        for zb in range(nodes):
            p_copy(t2, q, zb).wait_recv()
        if i < len(last) - 1:
            up_step(last[i], False)

    def hx_copy(t2, who_t, j):
        piece_ref = hid.at[who_t * 2 + p, j]
        return remote(piece_ref, piece_ref, hx_s.at[t2, j], hx_r.at[who_t, j], {"tensor": t2})

    def hp_copy(t2, core, j):
        piece_ref = hid.at[t2 * 2 + core, j]
        return remote(piece_ref, piece_ref, hp_s.at[t2, j], hp_r.at[t2, j], {"pair": q})

    if last:
        up_copy(last[-1]).wait()

    def hidden_step(j, carry):
        lanes = pl.ds(pl.multiple_of(j * chunk, chunk), chunk)
        value = acc[j]
        if last:
            value = value + up_part(last[-1], j)
        value = value * root_all + jnp.dot(mid, outmap_ref[:, lanes], preferred_element_type=F32)
        hid[c, j] = (value / (1.0 + jnp.exp(-value))).astype(BF16)
        for t2 in tens_to:
            hx_copy(t2, t, j).start()
        hp_copy(t, p, j).start()
        return carry

    lax.fori_loop(0, chunks, hidden_step, 0)

    def down_part(index, j):
        rows = pl.ds(pl.multiple_of(index * width + j * chunk, chunk), chunk)
        return jnp.dot(hid[index, j], w_down[rows, :], preferred_element_type=F32)

    down_copy(order[0]).wait()
    acc_down[...] = jnp.zeros_like(acc_down)

    def own_step(j, carry):
        acc_down[...] += down_part(c, j)
        return carry

    lax.fori_loop(0, chunks, own_step, 0)
    down_copy(order[1]).wait()

    def sibling_step(j, carry):
        hp_copy(t, q, j).wait_recv()
        acc_down[...] += down_part(t * 2 + q, j)
        return carry

    lax.fori_loop(0, chunks, sibling_step, 0)
    for t2 in tens_from:
        down_copy(t2 * 2 + p).wait()

        def across_step(j, carry, t2=t2):
            hx_copy(t2, t2, j).wait_recv()
            hp_copy(t2, p, j).start()
            acc_down[...] += down_part(t2 * 2 + p, j)
            return carry

        lax.fori_loop(0, chunks, across_step, 0)
    for t2 in tens_from:
        down_copy(t2 * 2 + q).wait()

        def diagonal_step(j, carry, t2=t2):
            hp_copy(t2, q, j).wait_recv()
            acc_down[...] += down_part(t2 * 2 + q, j)
            return carry

        lax.fori_loop(0, chunks, diagonal_step, 0)

    piece[...] = acc_down[...].astype(BF16)
    for z2 in node_to:
        go(remote(piece.at[at_block(z2)], ret.at[z], ret_s.at[z2], ret_r.at[z], {"node": z2}))

    def weight(node):
        expert = node // share
        return jnp.where(first_expert == expert, gate0, 0.0) + jnp.where(
            second_expert == expert, gate1, 0.0
        )

    mixed = head[...] + weight(z) * piece[at_block(z), :].astype(F32)
    for z2 in node_from:
        remote(ret.at[z2], ret.at[z2], ret_s.at[z2], ret_r.at[z2], {"node": z2}).wait_recv()
        mixed = mixed + weight(z2) * ret[z2].astype(F32)
    for index in range(groups):
        outb[index] = mixed[index * own : (index + 1) * own, :].astype(BF16)
    for c2 in chip_to:
        go(remote(outb.at[c2], out_ref.at[:, at_cols(c)], out_s.at[c2], out_r.at[c], to_chip(c2)))
    out_ref[:, at_cols(c)] = outb[c]
    for c2 in chip_from:
        remote(outb.at[c2], out_ref.at[:, at_cols(c2)], out_s.at[c2], out_r.at[c2], to_chip(c2)).wait_recv()

    for copy in sends:
        copy.wait_send()

    def drain(j, carry):
        for t2 in tens_to:
            hx_copy(t2, t, j).wait_send()
        hp_copy(t, p, j).wait_send()
        for t2 in tens_from:
            hp_copy(t2, p, j).wait_send()
        return carry

    lax.fori_loop(0, chunks, drain, 0)


def on_device(
    attention_partial,
    residual,
    norm_scale,
    router_matrix,
    up_matrix,
    down_matrix,
    adapter_in_maps,
    adapter_out_maps,
    token_experts,
    token_requests,
    request_adapters,
):
    nodes = lax.axis_size("node")
    tensors = lax.axis_size("tensor")
    groups = tensors * lax.axis_size("pair")
    share = nodes // EXPERT_COUNT
    own = residual.shape[2]
    block = attention_partial.shape[1]
    model = residual.shape[3]
    cols = model // groups
    width = up_matrix.shape[2]
    chunk = 512 if width % 512 == 0 else width
    chunks = width // chunk
    adapters, _, _, rank = adapter_in_maps.shape
    wide = adapters * rank
    tokens = nodes * block
    dims = (nodes, tensors, groups, own, block, cols, width, chunks, chunk, rank, adapters, share)
    in_columns = jnp.transpose(adapter_in_maps, (0, 1, 3, 2))
    vmem = pl.BlockSpec(memory_space=pltpu.VMEM)
    smem = pl.BlockSpec(memory_space=pltpu.SMEM)
    hbm = pl.BlockSpec(memory_space=pl.ANY)
    dma = pltpu.SemaphoreType.DMA
    mixed = pl.pallas_call(
        functools.partial(kernel, dims),
        out_shape=jax.ShapeDtypeStruct((own, model), BF16),
        in_specs=[hbm, vmem, vmem, vmem, hbm, hbm, hbm, vmem, smem, smem, smem],
        out_specs=vmem,
        scratch_shapes=[
            pltpu.VMEM((model, width), BF16),
            pltpu.VMEM((groups * width, cols), BF16),
            pltpu.VMEM((adapters, rank, cols), BF16),
            pltpu.VMEM((groups, block, cols), BF16),
            pltpu.VMEM((groups, own, cols), BF16),
            pltpu.VMEM((block, cols), F32),
            pltpu.VMEM((groups, tokens, cols), BF16),
            pltpu.VMEM((groups, 8, 128), jnp.int32),
            pltpu.VMEM((block, 128), jnp.int32),
            pltpu.VMEM((groups, block, 128), F32),
            pltpu.VMEM((nodes, block, 128), F32),
            pltpu.VMEM((groups, tokens, wide), BF16),
            pltpu.VMEM((chunks, tokens, chunk), F32),
            pltpu.VMEM((groups, chunks, tokens, chunk), BF16),
            pltpu.VMEM((tokens, cols), F32),
            pltpu.VMEM((tokens, cols), BF16),
            pltpu.VMEM((nodes, block, cols), BF16),
            pltpu.VMEM((groups, own, cols), BF16),
            dma((groups,)),
            dma((groups,)),
            dma((2,)),
            dma((groups,)),
            dma((groups,)),
            dma((groups,)),
            dma((groups,)),
            dma((groups,)),
            dma((groups,)),
            dma((groups,)),
            dma((groups,)),
            dma((nodes,)),
            dma((nodes,)),
            dma((nodes,)),
            dma((nodes,)),
            dma((tensors, nodes)),
            dma((tensors, nodes)),
            dma((tensors, nodes)),
            dma((tensors, nodes)),
            dma((groups,)),
            dma((groups,)),
            dma((tensors, chunks)),
            dma((tensors, chunks)),
            dma((tensors, chunks)),
            dma((tensors, chunks)),
            dma((nodes,)),
            dma((nodes,)),
            dma((groups,)),
            dma((groups,)),
        ],
        compiler_params=pltpu.CompilerParams(
            collective_id=0, has_side_effects=True, vmem_limit_bytes=60 * 1024 * 1024
        ),
        cost_estimate=pl.CostEstimate(
            flops=4 * tokens * model * width,
            bytes_accessed=4 * model * width,
            transcendentals=tokens * width,
        ),
    )(
        attention_partial[0],
        residual[0, 0],
        norm_scale[None, :],
        router_matrix.T,
        up_matrix[0],
        down_matrix[0],
        in_columns,
        adapter_out_maps.reshape(wide, width),
        token_experts[0, 0],
        token_requests[0, 0],
        request_adapters,
    )
    return mixed.reshape(1, 1, own, model)


def solution(mesh):
    in_specs = (
        P(("tensor", "pair"), ("groups", "node"), None),
        P(("groups", "node"), ("tensor", "pair"), None, None),
        P(),
        P(),
        P("node", None, ("tensor", "pair")),
        P("node", None, ("tensor", "pair")),
        P(None, None, ("tensor", "pair"), None),
        P(None, "node", None, ("tensor", "pair")),
        P(("groups", "node"), ("tensor", "pair"), None, None),
        P(("groups", "node"), ("tensor", "pair"), None),
        P("groups"),
    )
    out_specs = P(("groups", "node"), ("tensor", "pair"), None, None)
    return jax.shard_map(
        on_device, mesh=mesh, in_specs=in_specs, out_specs=out_specs, check_vma=False
    )
```

```python
import functools

import jax
import jax.numpy as jnp
from jax import lax
from jax.experimental import pallas as pl
from jax.experimental.pallas import tpu as pltpu
from jax.sharding import PartitionSpec as P

EXPERT_COUNT = 4
CAP = 3
MESH = pl.DeviceIdType.MESH
F32 = jnp.float32
BF16 = jnp.bfloat16


def kernel(
    dims,
    ap_ref,
    res_ref,
    scale_ref,
    router_ref,
    up_ref,
    down_ref,
    in_ref,
    outmap_ref,
    te_ref,
    tr_ref,
    ra_ref,
    out_ref,
    w_up,
    w_down,
    a_in,
    ap_buf,
    res_buf,
    head,
    y_buf,
    inf_buf,
    inf_all,
    part_buf,
    meta,
    lora_buf,
    acc,
    hid,
    acc_down,
    piece,
    ret,
    outb,
    scale_buf,
    up_sem,
    down_sem,
    loc_sem,
    ap_s,
    ap_r,
    res_s,
    res_r,
    inf_s,
    inf_r,
    part_s,
    part_r,
    meta_s,
    meta_r,
    z_s,
    z_r,
    x_s,
    x_r,
    p_s,
    p_r,
    lora_s,
    lora_r,
    hx_s,
    hx_r,
    hp_s,
    hp_r,
    ret_s,
    ret_r,
    out_s,
    out_r,
):
    nodes, tensors, groups, own, block, cols, width, chunks, chunk, rank, adapters, share, cap = dims
    z = lax.axis_index("node")
    t = lax.axis_index("tensor")
    p = lax.axis_index("pair")
    c = t * 2 + p
    q = 1 - p
    tokens = nodes * block

    def at_cols(index):
        return pl.ds(pl.multiple_of(index * cols, cols), cols)

    def at_block(index):
        return pl.ds(pl.multiple_of(index * block, block), block)

    def to_chip(index):
        return {"tensor": index // 2, "pair": lax.rem(index, 2)}

    def remote(src, dst, send, recv, device):
        return pltpu.make_async_remote_copy(
            src_ref=src, dst_ref=dst, send_sem=send, recv_sem=recv,
            device_id=device, device_id_type=MESH,
        )

    chip_to = [lax.rem(c + d, groups) for d in range(1, groups)]
    chip_from = [lax.rem(c - d + groups, groups) for d in range(1, groups)]
    node_to = [lax.rem(z + d, nodes) for d in range(1, nodes)]
    node_from = [lax.rem(z - d + nodes, nodes) for d in range(1, nodes)]
    tens_to = [lax.rem(t + d, tensors) for d in range(1, tensors)]
    tens_from = [lax.rem(t - d + tensors, tensors) for d in range(1, tensors)]
    sends = []

    def go(copy):
        copy.start()
        sends.append(copy)

    def up_copy(index):
        rows = at_cols(index)
        return pltpu.make_async_copy(up_ref.at[rows], w_up.at[rows], up_sem.at[index])

    def down_copy(index):
        rows = pl.ds(pl.multiple_of(index * width, width), width)
        return pltpu.make_async_copy(down_ref.at[rows], w_down.at[rows], down_sem.at[index])

    order = [c, t * 2 + q]
    for t2 in tens_from:
        order.append(t2 * 2 + p)
    for t2 in tens_from:
        order.append(t2 * 2 + q)

    barrier = pltpu.get_barrier_semaphore()
    for c2 in chip_to:
        pl.semaphore_signal(barrier, inc=1, device_id=to_chip(c2), device_id_type=MESH)
    for z2 in node_to:
        pl.semaphore_signal(barrier, inc=1, device_id={"node": z2}, device_id_type=MESH)

    own_ap = pltpu.make_async_copy(ap_ref.at[:, at_cols(c)], ap_buf.at[c], loc_sem.at[0])
    own_ap.start()
    in_copy = pltpu.make_async_copy(in_ref.at[:, z // share], a_in, loc_sem.at[1])
    in_copy.start()
    for index in order:
        up_copy(index).start()

    row8 = lax.broadcasted_iota(jnp.int32, (8, 128), 0)
    lane8 = lax.broadcasted_iota(jnp.int32, (8, 128), 1)
    info = jnp.zeros((8, 128), jnp.int32)
    for k in range(own):
        here = row8 == k
        info = jnp.where(here & (lane8 == 0), ra_ref[tr_ref[k]], info)
        info = jnp.where(here & (lane8 == 1), te_ref[0, k], info)
        info = jnp.where(here & (lane8 == 2), te_ref[1, k], info)
    inf_buf[c] = info

    pl.semaphore_wait(barrier, groups - 1 + nodes - 1)

    for c2 in chip_to:
        go(remote(ap_ref.at[:, at_cols(c2)], ap_buf.at[c], ap_s.at[c2], ap_r.at[c], to_chip(c2)))
    for c2 in chip_to:
        go(remote(res_ref.at[:, at_cols(c2)], res_buf.at[c], res_s.at[c2], res_r.at[c], to_chip(c2)))
    for c2 in chip_to:
        go(remote(inf_buf.at[c], inf_buf.at[c], inf_s.at[c2], inf_r.at[c], to_chip(c2)))

    res_buf[c] = res_ref[:, at_cols(c)]
    scale_buf[...] = scale_ref[...].astype(F32).reshape(1, groups * cols)
    for c2 in chip_from:
        remote(res_buf.at[c2], res_buf.at[c2], res_s.at[c2], res_r.at[c2], to_chip(c2)).wait_recv()
    for index in range(groups):
        head[index * own : (index + 1) * own, :] = res_buf[index].astype(F32)
    own_ap.wait()
    for c2 in chip_from:
        remote(ap_buf.at[c2], ap_buf.at[c2], ap_s.at[c2], ap_r.at[c2], to_chip(c2)).wait_recv()
    total = ap_buf[0].astype(F32)
    for index in range(1, groups):
        total = total + ap_buf[index].astype(F32)
    total = total + head[...]
    head[...] = total
    scale = scale_buf[:, at_cols(c)]
    y = (total * scale).astype(BF16)
    y_buf[c, at_block(z), :] = y

    def z_copy(z2, who):
        piece_ref = y_buf.at[c, at_block(who)]
        return remote(piece_ref, piece_ref, z_s.at[z2], z_r.at[who], {"node": z2})

    def x_copy(t2, who_t, zb):
        piece_ref = y_buf.at[who_t * 2 + p, at_block(zb)]
        return remote(piece_ref, piece_ref, x_s.at[t2, zb], x_r.at[who_t, zb], {"tensor": t2})

    def p_copy(t2, core, zb):
        piece_ref = y_buf.at[t2 * 2 + core, at_block(zb)]
        return remote(piece_ref, piece_ref, p_s.at[t2, zb], p_r.at[t2, zb], {"pair": q})

    def spread(zb):
        for t2 in tens_to:
            go(x_copy(t2, t, zb))
        go(p_copy(t, p, zb))

    for z2 in node_to:
        go(z_copy(z2, z))
    spread(z)

    lane = lax.broadcasted_iota(jnp.int32, (block, 128), 1)
    y32 = y.astype(F32)
    router = router_ref[:, at_cols(c)].astype(F32)
    partial = jnp.where(lane == 0, jnp.sum(total * total, axis=1, keepdims=True), 0.0)
    for e in range(EXPERT_COUNT):
        value = jnp.sum(y32 * router[e : e + 1, :], axis=1, keepdims=True)
        partial = jnp.where(lane == 1 + e, value, partial)
    part_buf[c] = partial
    for c2 in chip_to:
        go(remote(part_buf.at[c], part_buf.at[c], part_s.at[c2], part_r.at[c], to_chip(c2)))
    for index in order:
        down_copy(index).start()
    for z2 in node_from:
        z_copy(z2, z2).wait_recv()
        spread(z2)

    in_copy.wait()
    wide = adapters * rank
    mid = lax.dot_general(
        y_buf[c], a_in[...].reshape(wide, cols), (((1,), (1,)), ((), ())),
        preferred_element_type=F32,
    )
    lora_buf[c] = mid.astype(BF16)
    for c2 in chip_to:
        go(remote(lora_buf.at[c], lora_buf.at[c], lora_s.at[c2], lora_r.at[c], to_chip(c2)))

    for c2 in chip_from:
        remote(inf_buf.at[c2], inf_buf.at[c2], inf_s.at[c2], inf_r.at[c2], to_chip(c2)).wait_recv()
    for index in range(groups):
        inf_all[index * own : (index + 1) * own, :] = inf_buf[index, 0:own, :]
    for c2 in chip_from:
        remote(part_buf.at[c2], part_buf.at[c2], part_s.at[c2], part_r.at[c2], to_chip(c2)).wait_recv()
    sums = part_buf[0]
    for index in range(1, groups):
        sums = sums + part_buf[index]
    root = lax.rsqrt(sums[:, 0:1] / (groups * cols) + 1e-05)
    routes = inf_all[...]
    meta[z] = jnp.where(
        lane == 0,
        root,
        jnp.where(
            lane == 1,
            routes[:, 0:1].astype(F32),
            jnp.where(lane == 2, routes[:, 1:2], routes[:, 2:3]).astype(F32),
        ),
    )
    for z2 in node_to:
        go(remote(meta.at[z], meta.at[z], meta_s.at[z2], meta_r.at[z], {"node": z2}))
    first_expert = routes[:, 1:2]
    second_expert = routes[:, 2:3]
    chosen0 = jnp.zeros((block, 1), F32)
    chosen1 = jnp.zeros((block, 1), F32)
    for e in range(EXPERT_COUNT):
        logit = sums[:, 1 + e : 2 + e] * root
        chosen0 = jnp.where(first_expert == e, logit, chosen0)
        chosen1 = jnp.where(second_expert == e, logit, chosen1)
    gate0 = 1.0 / (1.0 + jnp.exp(chosen1 - chosen0))
    gate1 = 1.0 - gate0

    def up_part(index, j):
        lanes = pl.ds(pl.multiple_of(j * chunk, chunk), chunk)
        rows = at_cols(index)
        return jnp.dot(y_buf[index], w_up[rows, lanes], preferred_element_type=F32)

    def up_step(index, first):
        up_copy(index).wait()

        def body(j, carry):
            value = up_part(index, j)
            acc[j] = value if first else acc[j] + value
            return carry

        lax.fori_loop(0, chunks, body, 0)

    up_step(order[0], True)
    for zb in range(nodes):
        p_copy(t, q, zb).wait_recv()
    up_step(order[1], False)
    for t2 in tens_from:
        for zb in [z] + node_from:
            x_copy(t2, t2, zb).wait_recv()
            go(p_copy(t2, p, zb))
        up_step(t2 * 2 + p, False)

    for c2 in chip_from:
        remote(lora_buf.at[c2], lora_buf.at[c2], lora_s.at[c2], lora_r.at[c2], to_chip(c2)).wait_recv()
    for z2 in node_from:
        remote(meta.at[z2], meta.at[z2], meta_s.at[z2], meta_r.at[z2], {"node": z2}).wait_recv()
    facts = meta[...].reshape(tokens, 128)
    root_all = facts[:, 0:1]
    low = facts[:, 1:2] * float(rank)
    mid = lora_buf[0].astype(F32)
    for index in range(1, groups):
        mid = mid + lora_buf[index].astype(F32)
    slot = lax.broadcasted_iota(jnp.int32, (tokens, wide), 1).astype(F32)
    mid = jnp.where((slot >= low) & (slot < low + rank), mid * root_all, 0.0).astype(BF16)

    expert_here = (z // share).astype(F32)
    routed = jnp.where(
        (facts[:, 2:3] == expert_here) | (facts[:, 3:4] == expert_here), 1.0, 0.0
    )
    below = lax.broadcasted_iota(jnp.int32, (tokens, tokens), 0) > lax.broadcasted_iota(
        jnp.int32, (tokens, tokens), 1
    )
    place = jnp.dot(
        below.astype(F32).astype(BF16),
        jnp.broadcast_to(routed, (tokens, 128)).astype(BF16),
        preferred_element_type=F32,
    )[:, 0:1]
    slots = lax.broadcasted_iota(jnp.int32, (tokens, cap), 1).astype(F32)
    pack = jnp.where((routed > 0.0) & (slots == place), 1.0, 0.0).astype(BF16)

    last = [t2 * 2 + q for t2 in tens_from]
    for i, t2 in enumerate(tens_from):
        for zb in range(nodes):
            p_copy(t2, q, zb).wait_recv()
        if i < len(last) - 1:
            up_step(last[i], False)

    def hx_copy(t2, who_t, j):
        piece_ref = hid.at[who_t * 2 + p, j]
        return remote(piece_ref, piece_ref, hx_s.at[t2, j], hx_r.at[who_t, j], {"tensor": t2})

    def hp_copy(t2, core, j):
        piece_ref = hid.at[t2 * 2 + core, j]
        return remote(piece_ref, piece_ref, hp_s.at[t2, j], hp_r.at[t2, j], {"pair": q})

    if last:
        up_copy(last[-1]).wait()

    def hidden_step(j, carry):
        lanes = pl.ds(pl.multiple_of(j * chunk, chunk), chunk)
        value = acc[j]
        if last:
            value = value + up_part(last[-1], j)
        value = value * root_all + jnp.dot(mid, outmap_ref[:, lanes], preferred_element_type=F32)
        value = (value / (1.0 + jnp.exp(-value))).astype(BF16)
        hid[c, j] = lax.dot_general(
            pack, value, (((0,), (0,)), ((), ())), preferred_element_type=F32
        ).astype(BF16)
        for t2 in tens_to:
            hx_copy(t2, t, j).start()
        hp_copy(t, p, j).start()
        return carry

    lax.fori_loop(0, chunks, hidden_step, 0)

    def down_part(index, j):
        rows = pl.ds(pl.multiple_of(index * width + j * chunk, chunk), chunk)
        return jnp.dot(hid[index, j], w_down[rows, :], preferred_element_type=F32)

    down_copy(order[0]).wait()
    acc_down[...] = jnp.zeros_like(acc_down)

    def own_step(j, carry):
        acc_down[...] += down_part(c, j)
        return carry

    lax.fori_loop(0, chunks, own_step, 0)
    down_copy(order[1]).wait()

    def sibling_step(j, carry):
        hp_copy(t, q, j).wait_recv()
        acc_down[...] += down_part(t * 2 + q, j)
        return carry

    lax.fori_loop(0, chunks, sibling_step, 0)
    for t2 in tens_from:
        down_copy(t2 * 2 + p).wait()

        def across_step(j, carry, t2=t2):
            hx_copy(t2, t2, j).wait_recv()
            hp_copy(t2, p, j).start()
            acc_down[...] += down_part(t2 * 2 + p, j)
            return carry

        lax.fori_loop(0, chunks, across_step, 0)
    for t2 in tens_from:
        down_copy(t2 * 2 + q).wait()

        def diagonal_step(j, carry, t2=t2):
            hp_copy(t2, q, j).wait_recv()
            acc_down[...] += down_part(t2 * 2 + q, j)
            return carry

        lax.fori_loop(0, chunks, diagonal_step, 0)

    piece[...] = jnp.dot(
        pack, acc_down[...].astype(BF16), preferred_element_type=F32
    ).astype(BF16)
    for z2 in node_to:
        go(remote(piece.at[at_block(z2)], ret.at[z], ret_s.at[z2], ret_r.at[z], {"node": z2}))

    def weight(node):
        expert = node // share
        return jnp.where(first_expert == expert, gate0, 0.0) + jnp.where(
            second_expert == expert, gate1, 0.0
        )

    mixed = head[...] + weight(z) * piece[at_block(z), :].astype(F32)
    for z2 in node_from:
        remote(ret.at[z2], ret.at[z2], ret_s.at[z2], ret_r.at[z2], {"node": z2}).wait_recv()
        mixed = mixed + weight(z2) * ret[z2].astype(F32)
    for index in range(groups):
        outb[index] = mixed[index * own : (index + 1) * own, :].astype(BF16)
    for c2 in chip_to:
        go(remote(outb.at[c2], out_ref.at[:, at_cols(c)], out_s.at[c2], out_r.at[c], to_chip(c2)))
    out_ref[:, at_cols(c)] = outb[c]
    for c2 in chip_from:
        remote(outb.at[c2], out_ref.at[:, at_cols(c2)], out_s.at[c2], out_r.at[c2], to_chip(c2)).wait_recv()

    for copy in sends:
        copy.wait_send()

    def drain(j, carry):
        for t2 in tens_to:
            hx_copy(t2, t, j).wait_send()
        hp_copy(t, p, j).wait_send()
        for t2 in tens_from:
            hp_copy(t2, p, j).wait_send()
        return carry

    lax.fori_loop(0, chunks, drain, 0)


def on_device(
    attention_partial,
    residual,
    norm_scale,
    router_matrix,
    up_matrix,
    down_matrix,
    adapter_in_maps,
    adapter_out_maps,
    token_experts,
    token_requests,
    request_adapters,
):
    nodes = lax.axis_size("node")
    tensors = lax.axis_size("tensor")
    groups = tensors * lax.axis_size("pair")
    share = nodes // EXPERT_COUNT
    own = residual.shape[2]
    block = attention_partial.shape[1]
    model = residual.shape[3]
    cols = model // groups
    width = up_matrix.shape[2]
    chunk = 512 if width % 512 == 0 else width
    chunks = width // chunk
    adapters, _, _, rank = adapter_in_maps.shape
    wide = adapters * rank
    tokens = nodes * block
    cap = tokens // own * CAP
    dims = (nodes, tensors, groups, own, block, cols, width, chunks, chunk, rank, adapters, share, cap)
    in_columns = jnp.transpose(adapter_in_maps, (0, 1, 3, 2))
    vmem = pl.BlockSpec(memory_space=pltpu.VMEM)
    smem = pl.BlockSpec(memory_space=pltpu.SMEM)
    hbm = pl.BlockSpec(memory_space=pl.ANY)
    dma = pltpu.SemaphoreType.DMA
    mixed = pl.pallas_call(
        functools.partial(kernel, dims),
        out_shape=jax.ShapeDtypeStruct((own, model), BF16),
        in_specs=[hbm, vmem, vmem, vmem, hbm, hbm, hbm, vmem, smem, smem, smem],
        out_specs=vmem,
        scratch_shapes=[
            pltpu.VMEM((model, width), BF16),
            pltpu.VMEM((groups * width, cols), BF16),
            pltpu.VMEM((adapters, rank, cols), BF16),
            pltpu.VMEM((groups, block, cols), BF16),
            pltpu.VMEM((groups, own, cols), BF16),
            pltpu.VMEM((block, cols), F32),
            pltpu.VMEM((groups, tokens, cols), BF16),
            pltpu.VMEM((groups, 8, 128), jnp.int32),
            pltpu.VMEM((block, 128), jnp.int32),
            pltpu.VMEM((groups, block, 128), F32),
            pltpu.VMEM((nodes, block, 128), F32),
            pltpu.VMEM((groups, tokens, wide), BF16),
            pltpu.VMEM((chunks, tokens, chunk), F32),
            pltpu.VMEM((groups, chunks, cap, chunk), BF16),
            pltpu.VMEM((cap, cols), F32),
            pltpu.VMEM((tokens, cols), BF16),
            pltpu.VMEM((nodes, block, cols), BF16),
            pltpu.VMEM((groups, own, cols), BF16),
            pltpu.VMEM((1, model), F32),
            dma((groups,)),
            dma((groups,)),
            dma((2,)),
            dma((groups,)),
            dma((groups,)),
            dma((groups,)),
            dma((groups,)),
            dma((groups,)),
            dma((groups,)),
            dma((groups,)),
            dma((groups,)),
            dma((nodes,)),
            dma((nodes,)),
            dma((nodes,)),
            dma((nodes,)),
            dma((tensors, nodes)),
            dma((tensors, nodes)),
            dma((tensors, nodes)),
            dma((tensors, nodes)),
            dma((groups,)),
            dma((groups,)),
            dma((tensors, chunks)),
            dma((tensors, chunks)),
            dma((tensors, chunks)),
            dma((tensors, chunks)),
            dma((nodes,)),
            dma((nodes,)),
            dma((groups,)),
            dma((groups,)),
        ],
        compiler_params=pltpu.CompilerParams(
            collective_id=0, has_side_effects=True, vmem_limit_bytes=60 * 1024 * 1024
        ),
        cost_estimate=pl.CostEstimate(
            flops=4 * tokens * model * width,
            bytes_accessed=4 * model * width,
            transcendentals=tokens * width,
        ),
    )(
        attention_partial[0],
        residual[0, 0],
        norm_scale,
        router_matrix.T,
        up_matrix[0],
        down_matrix[0],
        in_columns,
        adapter_out_maps.reshape(wide, width),
        token_experts[0, 0].T,
        token_requests[0, 0],
        request_adapters,
    )
    return mixed.reshape(1, 1, own, model)


def solution(mesh):
    in_specs = (
        P(("tensor", "pair"), ("groups", "node"), None),
        P(("groups", "node"), ("tensor", "pair"), None, None),
        P(),
        P(),
        P("node", None, ("tensor", "pair")),
        P("node", None, ("tensor", "pair")),
        P(None, None, ("tensor", "pair"), None),
        P(None, "node", None, ("tensor", "pair")),
        P(("groups", "node"), ("tensor", "pair"), None, None),
        P(("groups", "node"), ("tensor", "pair"), None),
        P("groups"),
    )
    out_specs = P(("groups", "node"), ("tensor", "pair"), None, None)
    return jax.shard_map(
        on_device, mesh=mesh, in_specs=in_specs, out_specs=out_specs, check_vma=False
    )
```

```python
import functools

import jax
import jax.numpy as jnp
from jax import lax
from jax.experimental import pallas as pl
from jax.experimental.pallas import tpu as pltpu
from jax.sharding import PartitionSpec as P

EXPERT_COUNT = 4
CAP = 3
MESH = pl.DeviceIdType.MESH
F32 = jnp.float32
BF16 = jnp.bfloat16


def kernel(
    dims,
    ap_ref,
    res_ref,
    scale_ref,
    router_ref,
    up_ref,
    down_ref,
    in_ref,
    outmap_ref,
    te_ref,
    tr_ref,
    ra_ref,
    out_ref,
    w_up,
    w_down,
    a_in,
    ap_buf,
    res_buf,
    head,
    y_buf,
    inf_buf,
    inf_all,
    part_buf,
    meta,
    lora_buf,
    acc,
    hid,
    acc_down,
    piece,
    ret,
    outb,
    scale_buf,
    up_sem,
    down_sem,
    loc_sem,
    ap_s,
    ap_r,
    res_s,
    res_r,
    inf_s,
    inf_r,
    part_s,
    part_r,
    meta_s,
    meta_r,
    z_s,
    z_r,
    x_s,
    x_r,
    p_s,
    p_r,
    lora_s,
    lora_r,
    hx_s,
    hx_r,
    hp_s,
    hp_r,
    ret_s,
    ret_r,
    out_s,
    out_r,
):
    nodes, tensors, groups, own, block, cols, width, chunks, chunk, rank, adapters, share, cap = dims
    z = lax.axis_index("node")
    t = lax.axis_index("tensor")
    p = lax.axis_index("pair")
    c = t * 2 + p
    q = 1 - p
    tokens = nodes * block

    def at_cols(index):
        return pl.ds(pl.multiple_of(index * cols, cols), cols)

    def at_block(index):
        return pl.ds(pl.multiple_of(index * block, block), block)

    def to_chip(index):
        return {"tensor": index // 2, "pair": lax.rem(index, 2)}

    def remote(src, dst, send, recv, device):
        return pltpu.make_async_remote_copy(
            src_ref=src, dst_ref=dst, send_sem=send, recv_sem=recv,
            device_id=device, device_id_type=MESH,
        )

    chip_to = [lax.rem(c + d, groups) for d in range(1, groups)]
    chip_from = [lax.rem(c - d + groups, groups) for d in range(1, groups)]
    node_to = [lax.rem(z + d, nodes) for d in range(1, nodes)]
    node_from = [lax.rem(z - d + nodes, nodes) for d in range(1, nodes)]
    tens_to = [lax.rem(t + d, tensors) for d in range(1, tensors)]
    tens_from = [lax.rem(t - d + tensors, tensors) for d in range(1, tensors)]
    sends = []

    def go(copy):
        copy.start()
        sends.append(copy)

    def up_copy(index):
        rows = at_cols(index)
        return pltpu.make_async_copy(up_ref.at[rows], w_up.at[rows], up_sem.at[index])

    def down_copy(index):
        rows = pl.ds(pl.multiple_of(index * width, width), width)
        return pltpu.make_async_copy(down_ref.at[rows], w_down.at[rows], down_sem.at[index])

    order = [c, t * 2 + q]
    for t2 in tens_from:
        order.append(t2 * 2 + p)
    for t2 in tens_from:
        order.append(t2 * 2 + q)

    barrier = pltpu.get_barrier_semaphore()
    for c2 in chip_to:
        pl.semaphore_signal(barrier, inc=1, device_id=to_chip(c2), device_id_type=MESH)
    for z2 in node_to:
        pl.semaphore_signal(barrier, inc=1, device_id={"node": z2}, device_id_type=MESH)

    own_ap = pltpu.make_async_copy(ap_ref.at[:, at_cols(c)], ap_buf.at[c], loc_sem.at[0])
    own_ap.start()
    in_copy = pltpu.make_async_copy(in_ref.at[:, z // share], a_in, loc_sem.at[1])
    in_copy.start()
    for index in order:
        up_copy(index).start()

    row8 = lax.broadcasted_iota(jnp.int32, (8, 128), 0)
    lane8 = lax.broadcasted_iota(jnp.int32, (8, 128), 1)
    info = jnp.zeros((8, 128), jnp.int32)
    for k in range(own):
        here = row8 == k
        info = jnp.where(here & (lane8 == 0), ra_ref[tr_ref[k]], info)
        info = jnp.where(here & (lane8 == 1), te_ref[0, k], info)
        info = jnp.where(here & (lane8 == 2), te_ref[1, k], info)
    inf_buf[c] = info

    pl.semaphore_wait(barrier, groups - 1 + nodes - 1)

    for c2 in chip_to:
        go(remote(ap_ref.at[:, at_cols(c2)], ap_buf.at[c], ap_s.at[c2], ap_r.at[c], to_chip(c2)))
    for c2 in chip_to:
        go(remote(res_ref.at[:, at_cols(c2)], res_buf.at[c], res_s.at[c2], res_r.at[c], to_chip(c2)))
    for c2 in chip_to:
        go(remote(inf_buf.at[c], inf_buf.at[c], inf_s.at[c2], inf_r.at[c], to_chip(c2)))

    res_buf[c] = res_ref[:, at_cols(c)]
    scale_buf[...] = scale_ref[...].astype(F32).reshape(1, groups * cols)
    for c2 in chip_from:
        remote(res_buf.at[c2], res_buf.at[c2], res_s.at[c2], res_r.at[c2], to_chip(c2)).wait_recv()
    for index in range(groups):
        head[index * own : (index + 1) * own, :] = res_buf[index].astype(F32)
    own_ap.wait()
    for c2 in chip_from:
        remote(ap_buf.at[c2], ap_buf.at[c2], ap_s.at[c2], ap_r.at[c2], to_chip(c2)).wait_recv()
    total = ap_buf[0].astype(F32)
    for index in range(1, groups):
        total = total + ap_buf[index].astype(F32)
    total = total + head[...]
    head[...] = total
    scale = scale_buf[:, at_cols(c)]
    y = (total * scale).astype(BF16)
    y_buf[c, at_block(z), :] = y

    def z_copy(z2, who):
        piece_ref = y_buf.at[c, at_block(who)]
        return remote(piece_ref, piece_ref, z_s.at[z2], z_r.at[who], {"node": z2})

    def x_copy(t2, who_t, zb):
        piece_ref = y_buf.at[who_t * 2 + p, at_block(zb)]
        return remote(piece_ref, piece_ref, x_s.at[t2, zb], x_r.at[who_t, zb], {"tensor": t2})

    def p_copy(t2, core, zb):
        piece_ref = y_buf.at[t2 * 2 + core, at_block(zb)]
        return remote(piece_ref, piece_ref, p_s.at[t2, zb], p_r.at[t2, zb], {"pair": q})

    def spread(zb):
        for t2 in tens_to:
            go(x_copy(t2, t, zb))
        go(p_copy(t, p, zb))

    for z2 in node_to:
        go(z_copy(z2, z))
    spread(z)

    lane = lax.broadcasted_iota(jnp.int32, (block, 128), 1)
    y32 = y.astype(F32)
    router = router_ref[:, at_cols(c)].astype(F32)
    partial = jnp.where(lane == 0, jnp.sum(total * total, axis=1, keepdims=True), 0.0)
    for e in range(EXPERT_COUNT):
        value = jnp.sum(y32 * router[e : e + 1, :], axis=1, keepdims=True)
        partial = jnp.where(lane == 1 + e, value, partial)
    part_buf[c] = partial
    for c2 in chip_to:
        go(remote(part_buf.at[c], part_buf.at[c], part_s.at[c2], part_r.at[c], to_chip(c2)))
    for index in order:
        down_copy(index).start()
    for z2 in node_from:
        z_copy(z2, z2).wait_recv()
        spread(z2)

    in_copy.wait()
    wide = adapters * rank
    mid = lax.dot_general(
        y_buf[c], a_in[...].reshape(wide, cols), (((1,), (1,)), ((), ())),
        preferred_element_type=F32,
    )
    lora_buf[c] = mid.astype(BF16)
    for c2 in chip_to:
        go(remote(lora_buf.at[c], lora_buf.at[c], lora_s.at[c2], lora_r.at[c], to_chip(c2)))

    for c2 in chip_from:
        remote(inf_buf.at[c2], inf_buf.at[c2], inf_s.at[c2], inf_r.at[c2], to_chip(c2)).wait_recv()
    for index in range(groups):
        inf_all[index * own : (index + 1) * own, :] = inf_buf[index, 0:own, :]
    for c2 in chip_from:
        remote(part_buf.at[c2], part_buf.at[c2], part_s.at[c2], part_r.at[c2], to_chip(c2)).wait_recv()
    sums = part_buf[0]
    for index in range(1, groups):
        sums = sums + part_buf[index]
    root = lax.rsqrt(sums[:, 0:1] / (groups * cols) + 1e-05)
    routes = inf_all[...]
    meta[z] = jnp.where(
        lane == 0,
        root,
        jnp.where(
            lane == 1,
            routes[:, 0:1].astype(F32),
            jnp.where(lane == 2, routes[:, 1:2], routes[:, 2:3]).astype(F32),
        ),
    )
    for z2 in node_to:
        go(remote(meta.at[z], meta.at[z], meta_s.at[z2], meta_r.at[z], {"node": z2}))
    first_expert = routes[:, 1:2]
    second_expert = routes[:, 2:3]
    chosen0 = jnp.zeros((block, 1), F32)
    chosen1 = jnp.zeros((block, 1), F32)
    for e in range(EXPERT_COUNT):
        logit = sums[:, 1 + e : 2 + e] * root
        chosen0 = jnp.where(first_expert == e, logit, chosen0)
        chosen1 = jnp.where(second_expert == e, logit, chosen1)
    gate0 = 1.0 / (1.0 + jnp.exp(chosen1 - chosen0))
    gate1 = 1.0 - gate0

    def up_part(index, j):
        lanes = pl.ds(pl.multiple_of(j * chunk, chunk), chunk)
        rows = at_cols(index)
        return jnp.dot(y_buf[index], w_up[rows, lanes], preferred_element_type=F32)

    def up_step(index, first):
        up_copy(index).wait()

        def body(j, carry):
            value = up_part(index, j)
            acc[j] = value if first else acc[j] + value
            return carry

        lax.fori_loop(0, chunks, body, 0)

    up_step(order[0], True)
    for zb in range(nodes):
        p_copy(t, q, zb).wait_recv()
    up_step(order[1], False)
    for t2 in tens_from:
        for zb in [z] + node_from:
            x_copy(t2, t2, zb).wait_recv()
            go(p_copy(t2, p, zb))
        up_step(t2 * 2 + p, False)

    for c2 in chip_from:
        remote(lora_buf.at[c2], lora_buf.at[c2], lora_s.at[c2], lora_r.at[c2], to_chip(c2)).wait_recv()
    for z2 in node_from:
        remote(meta.at[z2], meta.at[z2], meta_s.at[z2], meta_r.at[z2], {"node": z2}).wait_recv()
    facts = meta[...].reshape(tokens, 128)
    root_all = facts[:, 0:1]
    low = facts[:, 1:2] * float(rank)
    mid = lora_buf[0].astype(F32)
    for index in range(1, groups):
        mid = mid + lora_buf[index].astype(F32)
    slot = lax.broadcasted_iota(jnp.int32, (tokens, wide), 1).astype(F32)
    mid = jnp.where((slot >= low) & (slot < low + rank), mid * root_all, 0.0).astype(BF16)

    expert_here = (z // share).astype(F32)
    routed = jnp.where(
        (facts[:, 2:3] == expert_here) | (facts[:, 3:4] == expert_here), 1.0, 0.0
    )
    below = lax.broadcasted_iota(jnp.int32, (tokens, tokens), 0) > lax.broadcasted_iota(
        jnp.int32, (tokens, tokens), 1
    )
    place = jnp.dot(
        below.astype(F32).astype(BF16),
        jnp.broadcast_to(routed, (tokens, 128)).astype(BF16),
        preferred_element_type=F32,
    )[:, 0:1]
    slots = lax.broadcasted_iota(jnp.int32, (tokens, cap), 1).astype(F32)
    pack = jnp.where((routed > 0.0) & (slots == place), 1.0, 0.0).astype(BF16)

    last = [t2 * 2 + q for t2 in tens_from]
    for i, t2 in enumerate(tens_from):
        for zb in range(nodes):
            p_copy(t2, q, zb).wait_recv()
        if i < len(last) - 1:
            up_step(last[i], False)

    def hx_copy(t2, who_t, j):
        piece_ref = hid.at[who_t * 2 + p, j]
        return remote(piece_ref, piece_ref, hx_s.at[t2, j], hx_r.at[who_t, j], {"tensor": t2})

    def hp_copy(t2, core, j):
        piece_ref = hid.at[t2 * 2 + core, j]
        return remote(piece_ref, piece_ref, hp_s.at[t2, j], hp_r.at[t2, j], {"pair": q})

    if last:
        up_copy(last[-1]).wait()

    def hidden_step(j, carry):
        lanes = pl.ds(pl.multiple_of(j * chunk, chunk), chunk)
        value = acc[j]
        if last:
            value = value + up_part(last[-1], j)
        value = value * root_all + jnp.dot(mid, outmap_ref[:, lanes], preferred_element_type=F32)
        value = (value / (1.0 + jnp.exp(-value))).astype(BF16)
        hid[c, j] = lax.dot_general(
            pack, value, (((0,), (0,)), ((), ())), preferred_element_type=F32
        ).astype(BF16)
        for t2 in tens_to:
            hx_copy(t2, t, j).start()
        hp_copy(t, p, j).start()
        return carry

    lax.fori_loop(0, chunks, hidden_step, 0)

    def down_part(index, j):
        rows = pl.ds(pl.multiple_of(index * width + j * chunk, chunk), chunk)
        return jnp.dot(hid[index, j], w_down[rows, :], preferred_element_type=F32)

    down_copy(order[0]).wait()
    acc_down[...] = jnp.zeros_like(acc_down)

    def own_step(j, carry):
        acc_down[...] += down_part(c, j)
        return carry

    lax.fori_loop(0, chunks, own_step, 0)
    down_copy(order[1]).wait()

    def sibling_step(j, carry):
        hp_copy(t, q, j).wait_recv()
        acc_down[...] += down_part(t * 2 + q, j)
        return carry

    lax.fori_loop(0, chunks, sibling_step, 0)
    for t2 in tens_from:
        down_copy(t2 * 2 + p).wait()

        def across_step(j, carry, t2=t2):
            hx_copy(t2, t2, j).wait_recv()
            hp_copy(t2, p, j).start()
            acc_down[...] += down_part(t2 * 2 + p, j)
            return carry

        lax.fori_loop(0, chunks, across_step, 0)
    for t2 in tens_from:
        down_copy(t2 * 2 + q).wait()

        def diagonal_step(j, carry, t2=t2):
            hp_copy(t2, q, j).wait_recv()
            acc_down[...] += down_part(t2 * 2 + q, j)
            return carry

        lax.fori_loop(0, chunks, diagonal_step, 0)

    piece[...] = jnp.dot(
        pack, acc_down[...].astype(BF16), preferred_element_type=F32
    ).astype(BF16)
    for z2 in node_to:
        go(remote(piece.at[at_block(z2)], ret.at[z], ret_s.at[z2], ret_r.at[z], {"node": z2}))

    def weight(node):
        expert = node // share
        return jnp.where(first_expert == expert, gate0, 0.0) + jnp.where(
            second_expert == expert, gate1, 0.0
        )

    mixed = head[...] + weight(z) * piece[at_block(z), :].astype(F32)
    for z2 in node_from:
        remote(ret.at[z2], ret.at[z2], ret_s.at[z2], ret_r.at[z2], {"node": z2}).wait_recv()
        mixed = mixed + weight(z2) * ret[z2].astype(F32)
    for index in range(groups):
        outb[index] = mixed[index * own : (index + 1) * own, :].astype(BF16)
    for c2 in chip_to:
        go(remote(outb.at[c2], out_ref.at[:, at_cols(c)], out_s.at[c2], out_r.at[c], to_chip(c2)))
    out_ref[:, at_cols(c)] = outb[c]
    for c2 in chip_from:
        remote(outb.at[c2], out_ref.at[:, at_cols(c2)], out_s.at[c2], out_r.at[c2], to_chip(c2)).wait_recv()

    for copy in sends:
        copy.wait_send()

    def drain(j, carry):
        for t2 in tens_to:
            hx_copy(t2, t, j).wait_send()
        hp_copy(t, p, j).wait_send()
        for t2 in tens_from:
            hp_copy(t2, p, j).wait_send()
        return carry

    lax.fori_loop(0, chunks, drain, 0)


def on_device(
    attention_partial,
    residual,
    norm_scale,
    router_matrix,
    up_matrix,
    down_matrix,
    adapter_in_maps,
    adapter_out_maps,
    token_experts,
    token_requests,
    request_adapters,
):
    nodes = lax.axis_size("node")
    tensors = lax.axis_size("tensor")
    groups = tensors * lax.axis_size("pair")
    share = nodes // EXPERT_COUNT
    own = residual.shape[2]
    block = attention_partial.shape[1]
    model = residual.shape[3]
    cols = model // groups
    width = up_matrix.shape[2]
    chunk = 1024 if width % 1024 == 0 else width
    chunks = width // chunk
    adapters, _, _, rank = adapter_in_maps.shape
    wide = adapters * rank
    tokens = nodes * block
    cap = tokens // own * CAP
    dims = (nodes, tensors, groups, own, block, cols, width, chunks, chunk, rank, adapters, share, cap)
    in_columns = jnp.transpose(adapter_in_maps, (0, 1, 3, 2))
    vmem = pl.BlockSpec(memory_space=pltpu.VMEM)
    smem = pl.BlockSpec(memory_space=pltpu.SMEM)
    hbm = pl.BlockSpec(memory_space=pl.ANY)
    dma = pltpu.SemaphoreType.DMA
    mixed = pl.pallas_call(
        functools.partial(kernel, dims),
        out_shape=jax.ShapeDtypeStruct((own, model), BF16),
        in_specs=[hbm, vmem, vmem, vmem, hbm, hbm, hbm, vmem, smem, smem, smem],
        out_specs=vmem,
        scratch_shapes=[
            pltpu.VMEM((model, width), BF16),
            pltpu.VMEM((groups * width, cols), BF16),
            pltpu.VMEM((adapters, rank, cols), BF16),
            pltpu.VMEM((groups, block, cols), BF16),
            pltpu.VMEM((groups, own, cols), BF16),
            pltpu.VMEM((block, cols), F32),
            pltpu.VMEM((groups, tokens, cols), BF16),
            pltpu.VMEM((groups, 8, 128), jnp.int32),
            pltpu.VMEM((block, 128), jnp.int32),
            pltpu.VMEM((groups, block, 128), F32),
            pltpu.VMEM((nodes, block, 128), F32),
            pltpu.VMEM((groups, tokens, wide), BF16),
            pltpu.VMEM((chunks, tokens, chunk), F32),
            pltpu.VMEM((groups, chunks, cap, chunk), BF16),
            pltpu.VMEM((cap, cols), F32),
            pltpu.VMEM((tokens, cols), BF16),
            pltpu.VMEM((nodes, block, cols), BF16),
            pltpu.VMEM((groups, own, cols), BF16),
            pltpu.VMEM((1, model), F32),
            dma((groups,)),
            dma((groups,)),
            dma((2,)),
            dma((groups,)),
            dma((groups,)),
            dma((groups,)),
            dma((groups,)),
            dma((groups,)),
            dma((groups,)),
            dma((groups,)),
            dma((groups,)),
            dma((nodes,)),
            dma((nodes,)),
            dma((nodes,)),
            dma((nodes,)),
            dma((tensors, nodes)),
            dma((tensors, nodes)),
            dma((tensors, nodes)),
            dma((tensors, nodes)),
            dma((groups,)),
            dma((groups,)),
            dma((tensors, chunks)),
            dma((tensors, chunks)),
            dma((tensors, chunks)),
            dma((tensors, chunks)),
            dma((nodes,)),
            dma((nodes,)),
            dma((groups,)),
            dma((groups,)),
        ],
        compiler_params=pltpu.CompilerParams(
            collective_id=0, has_side_effects=True, vmem_limit_bytes=60 * 1024 * 1024
        ),
        cost_estimate=pl.CostEstimate(
            flops=4 * tokens * model * width,
            bytes_accessed=4 * model * width,
            transcendentals=tokens * width,
        ),
    )(
        attention_partial[0],
        residual[0, 0],
        norm_scale,
        router_matrix.T,
        up_matrix[0],
        down_matrix[0],
        in_columns,
        adapter_out_maps.reshape(wide, width),
        token_experts[0, 0].T,
        token_requests[0, 0],
        request_adapters,
    )
    return mixed.reshape(1, 1, own, model)


def solution(mesh):
    in_specs = (
        P(("tensor", "pair"), ("groups", "node"), None),
        P(("groups", "node"), ("tensor", "pair"), None, None),
        P(),
        P(),
        P("node", None, ("tensor", "pair")),
        P("node", None, ("tensor", "pair")),
        P(None, None, ("tensor", "pair"), None),
        P(None, "node", None, ("tensor", "pair")),
        P(("groups", "node"), ("tensor", "pair"), None, None),
        P(("groups", "node"), ("tensor", "pair"), None),
        P("groups"),
    )
    out_specs = P(("groups", "node"), ("tensor", "pair"), None, None)
    return jax.shard_map(
        on_device, mesh=mesh, in_specs=in_specs, out_specs=out_specs, check_vma=False
    )
```
